256 devices in a mesh: dp: 32 (over x, z_lo, core), shard: 8 (over z_hi, y).
Axes of the slice: x: 4, y: 4, z: 8 (z_hi: 2, z_lo: 4; z = z_hi * 4 + z_lo), core: 2. Of those that a mesh axis runs over, the one named last changes fastest.
Arguments:
- grads: bfloat16 [32, 32, 704, 2048], P('dp', None, None, 'shard'), may hold values from -6 to 6
- mantissa: bfloat16 [32, 704, 2048], P(None, 'dp', 'shard'), may hold values from -4 to 4
- exponents: int32 [32, 704, 64], P(None, 'dp', 'shard'), may hold values from -2 to 1
Outputs:
- update: bfloat16 [32, 704, 2048], P(None, 'dp', 'shard')
- momentum: float32 [32, 704, 2048], P(None, 'dp', 'shard')
The draws below stay inside these ranges and needn't reach their ends.
Inputs may be any that keep to these rules, and one draw needn't show every extreme that they name: exponents[m, r, b] scales columns b * 32 to b * 32 + 31 of row r of matrix m.
All inputs are finite; a program needn't handle non-finite values.
Results may differ from the reference program's by a relative error of at most 0.028.
Values may be sent and summed in bfloat16 or wider, within the bound.
No kernel may reach another device: no remote copies, remote signals or barrier semaphores. Data moves between devices by JAX's collectives and lax.ppermute only.
A program may use at most 128 MiB of HBM per device.

```python
import math
import jax
import jax.numpy as jnp
from jax import lax

D = 2048
FW = 704
BLK = 32
ITERS = 3
MATS = 32
N_DP = 32


def plant(values, key, least, high):
    longest = values.shape.index(max(values.shape))
    spots = []
    for shift in (0, 1):
        where = [jax.random.randint(jax.random.fold_in(key, axis), (), 0, length) for axis, length in enumerate(values.shape)]
        where[longest] = (where[longest] + shift) % values.shape[longest]
        spots.append(tuple(where))
    return values.at[spots[0]].set(least).at[spots[1]].set(high)


def spiked(values, rng, source, target, shards_of, factor):
    def block_of(axis_at):
        return (jnp.arange(values.shape[axis_at]) // (values.shape[axis_at] // shards_of)).reshape((-1,) + (1,) * (values.ndim - 1 - axis_at))

    near = jax.random.permutation(rng, shards_of)[block_of(target)]
    second = (block_of(target) + shards_of // 2) % shards_of
    return jnp.where((block_of(source) == near) | (block_of(source) == second), factor * values, values)


def block_scale(stream_key, shape, shards, low, largest):
    level, own = 1.0, jax.random.fold_in(stream_key, 6)
    for axis_at, parts in shards:
        draws = jnp.exp(jax.random.uniform(jax.random.fold_in(own, axis_at), (parts,), jnp.float32, low / len(shards), largest / len(shards)))
        level = level * jnp.repeat(draws, shape[axis_at] // parts).reshape([-1 if axis == axis_at else 1 for axis in range(len(shape))])
    return level


def centred(stream_key, shape, deviation, reach, split=(), held_as=jnp.bfloat16):
    drawn = deviation * jax.random.normal(stream_key, shape, jnp.float32)
    if split:
        drawn = drawn * block_scale(stream_key, shape, split, -0.22, 0.18)
    return jnp.clip(drawn, -reach, reach).astype(held_as)


def bell_draw_with(rng, extent, width, limit, pieces, heavy, held_as=jnp.bfloat16):
    drawn = width * jax.random.normal(rng, extent, jnp.float32)
    if pieces:
        drawn = drawn * block_scale(rng, extent, pieces, -0.22, 0.18)
    return jnp.clip(spiked(drawn, jax.random.fold_in(rng, 3), *heavy), -limit, limit).astype(held_as)


def setup_inputs(seed: int = 0) -> dict:
    key_of = jax.random.split(jax.random.key(seed), 4)
    return {
        "grads": bell_draw_with(key_of[0], (N_DP, MATS, FW, D), 1.0, 6.0, ((0, 32), (3, 8)), (0, 2, 32, 2.75)),
        "mantissa": centred(key_of[1], (MATS, FW, D), 0.5, 4.0, ((1, 32), (2, 8))),
        "exponents": plant(jax.random.randint(key_of[2], (MATS, FW, D // BLK), -2, 2), jax.random.fold_in(key_of[2], 1), -2, 1).astype(jnp.int32),
    }


coef_a = 3.4445
coef_b = -4.775
coef_c = 2.0315
momentum_beta = 0.95
epsilon = 1e-07

def orthogonalize(nesterov):
    as_float = nesterov.astype(jnp.float32)
    norm_value = jnp.sqrt(jnp.sum(as_float * as_float))
    current = (as_float / (norm_value + epsilon)).astype(jnp.bfloat16)
    for iteration in range(ITERS):
        gram = jnp.dot(current, current.T, preferred_element_type=jnp.float32).astype(jnp.bfloat16)
        square = jnp.dot(gram, gram, preferred_element_type=jnp.float32)
        mixing = (coef_b * gram.astype(jnp.float32) + coef_c * square).astype(jnp.bfloat16)
        current = (coef_a * current.astype(jnp.float32) + jnp.dot(mixing, current, preferred_element_type=jnp.float32)).astype(jnp.bfloat16)
    return current

def reference(grads, mantissa, exponents):
    scale_factor = 0.2 * math.sqrt(max(D, FW))

    def single_matrix(matrix_index):
        picked = lax.dynamic_index_in_dim(grads, matrix_index, 1, keepdims=False)
        summed = lax.optimization_barrier(jnp.sum(picked.astype(jnp.float32), axis=0)) / N_DP
        block_exp = lax.dynamic_index_in_dim(exponents, matrix_index, 0, keepdims=False)
        scales = jnp.repeat(jnp.exp2(block_exp.astype(jnp.float32)), BLK, axis=1)
        values = lax.dynamic_index_in_dim(mantissa, matrix_index, 0, keepdims=False)
        momentum = momentum_beta * values.astype(jnp.float32) * scales + summed
        nesterov = (summed + momentum_beta * momentum).astype(jnp.bfloat16)
        result = orthogonalize(nesterov)
        update = (scale_factor * result.astype(jnp.float32)).astype(jnp.bfloat16)
        return (update, momentum)
    updates, moments = lax.map(single_matrix, jnp.arange(MATS, dtype=jnp.int32))
    return (updates, moments)
```

```python
import math

import jax
import jax.numpy as jnp
from jax import lax
from jax.experimental import pallas as pl
from jax.experimental.pallas import tpu as pltpu
from jax.sharding import PartitionSpec as P

D = 2048
FW = 704
BLK = 32
ITERS = 3

coef_a = 3.4445
coef_b = -4.775
coef_c = 2.0315
momentum_beta = 0.95
epsilon = 1e-07
bf16 = jnp.bfloat16
f32 = jnp.float32

CHUNKS = (144, 160, 48)
STARTS = [2 * sum(CHUNKS[:n]) for n in range(len(CHUNKS))]
PAD = 768
JOIN = momentum_beta * momentum_beta / (1 + momentum_beta)
WINDOW = 64


def dp_moves(move):
    pairs = []
    for x in range(4):
        for z in range(4):
            for core in range(2):
                nx, nz, nc = move(x, z, core)
                pairs.append((x * 8 + z * 2 + core, nx * 8 + nz * 2 + nc))
    return pairs


CORE = dp_moves(lambda x, z, core: (x, z, 1 - core))
X = {k: dp_moves(lambda x, z, core, k=k: (x ^ k, z, core)) for k in (1, 3)}
Z = {k: dp_moves(lambda x, z, core, k=k: (x, z ^ k, core)) for k in (1, 2)}
Y = {k: [(s, s ^ k) for s in range(8)] for k in (1, 2, 3, 4)}


def add(*terms):
    total = terms[0].astype(f32)
    for term in terms[1:]:
        total = total + term.astype(f32)
    return total


LARGE = 50 * 2**20
VMEM = 14 * 2**20


def call(body, place, operands, outs, scratch, flops=0, vmem=VMEM):
    return pl.pallas_call(
        body,
        out_shape=[jax.ShapeDtypeStruct(shape, bf16) for shape in outs],
        in_specs=[pl.BlockSpec(memory_space=pltpu.SMEM)] + [pl.BlockSpec(memory_space=pl.ANY)] * len(operands),
        out_specs=[pl.BlockSpec(memory_space=pltpu.VMEM)] * len(outs),
        scratch_shapes=scratch,
        compiler_params=pltpu.CompilerParams(vmem_limit_bytes=vmem),
        cost_estimate=pl.CostEstimate(flops=flops, bytes_accessed=6000000, transcendentals=0),
    )(place, *operands)


def begin(pairs, sems):
    copies = [pltpu.make_async_copy(source, target, sems.at[n]) for n, (source, target) in enumerate(pairs)]
    for copy in copies:
        copy.start()
    return copies


def finish(copies):
    for copy in copies:
        copy.wait()


def core_rows(place, grads, n):
    rows = 2 * CHUNKS[n]

    def body(place, grads, out, sems):
        there = pl.ds(STARTS[n], rows)
        finish(begin([(grads.at[x, :, 1 - place[2], there], out.at[x]) for x in range(4)], sems))

    return call(body, place, (grads,), [(4, 4, rows, 256)], [pltpu.SemaphoreType.DMA((4,))], vmem=LARGE)


def tree_add(terms):
    while len(terms) > 1:
        terms = [sum(terms[n + 1 : n + 2], terms[n]) for n in range(0, len(terms), 2)]
    return terms[0]


def sums_kernel(place, grads, joined, arrived, others, outs, jobs, start, rows, along_x=False):
    count = len(jobs)
    terms = 2 + max(len(job[2]) for job in jobs)

    def body(place, grads, joined, arrived, *refs):
        others_in, refs = refs[: len(others)], refs[len(others) :]
        outs_ref, (buffers, window, sems) = refs[: len(outs)], refs[len(outs) :]
        x, z, core = place[0], place[1], place[2]
        reads = []
        for n, (k, first, extra, _) in enumerate(jobs):
            which = (slice(None), z ^ k) if along_x else (x ^ k, slice(None))
            pairs = [
                (grads.at[(*which, core, pl.ds(start + first, rows))], buffers.at[n, 0]),
                (joined.at[which], window.at[n]),
                (arrived.at[(*which, pl.ds(first, rows))], buffers.at[n, 1]),
            ]
            pairs += [(term(others_in), buffers.at[n, 2 + t]) for t, term in enumerate(extra)]
            reads.append(begin(pairs, sems.at[n]))
        for n, (k, first, extra, store) in enumerate(jobs):
            finish(reads[n])
            for i in range(WINDOW // 16):
                at = place[4] + 16 * i - start - first

                @pl.when((at >= 0) & (at < rows))
                def _(n=n, i=i, at=at):
                    there = pl.ds(pl.multiple_of(at, 16), 16)
                    buffers[n, 0, :, there] = add(buffers[n, 0, :, there], window[n, :, 16 * i : 16 * i + 16]).astype(bf16)

            store(outs_ref, lambda j: tree_add([buffers[n, t, j] for t in range(2 + len(extra))]), x, z)

    return call(
        body, place, (grads, joined, arrived, *others), outs,
        [
            pltpu.VMEM((count, terms, 4, rows, 256), bf16),
            pltpu.VMEM((count, 4, WINDOW, 256), bf16),
            pltpu.SemaphoreType.DMA((count, terms + 1)),
        ],
        vmem=LARGE,
    )


def first_sends(place, grads, joined, arrived, n):
    half = CHUNKS[n]

    def job(k, part, slot):
        def store(outs, value, x, z):
            for j in range(4):
                outs[part][slot, j] = value(j)

        return (k, part * half, [], store)

    jobs = [job(2, 0, 1), job(1, 0, 0), job(2, 1, 1), job(3, 1, 0)]
    return sums_kernel(place, grads, joined, arrived, (), [(2, 4, half, 256)] * 2, jobs, STARTS[n], half)


def second_sends(place, grads, joined, arrived, got, n):
    half = CHUNKS[n]

    def job(k, part):
        def store(outs, value, x, z):
            for j in range(4):
                outs[part][j] = value(j)

        return (k, part * half, [lambda refs: refs[part].at[1]], store)

    return sums_kernel(
        place, grads, joined, arrived, got, [(4, half, 256)] * 2, [job(3, 0), job(1, 1)], STARTS[n], half
    )


def z_sends(place, grads, joined, arrived, got, last, n):
    half = CHUNKS[n]

    def job(part):
        def store(outs, value, x, z):
            rows = slice(part * half, part * half + half)
            for out, slot, k in ((0, 0, 1), (0, 1, 3), (1, 0, 0), (1, 1, 2)):
                outs[out][slot, rows] = value(z ^ k)

        return (0, part * half, [lambda refs: refs[part].at[0], lambda refs: refs[2 + part]], store)

    return sums_kernel(
        place, grads, joined, arrived, (*got, *last), [(2, 2 * half, 256)] * 2, [job(0), job(1)], STARTS[n], half
    )


def z_first_sends(place, grads, joined, arrived, n):
    def job(k, slot):
        def store(outs, value, x, z):
            for j in range(4):
                outs[0][slot, j] = value(j)

        return (k, 0, [], store)

    rows = 2 * CHUNKS[n]
    return sums_kernel(
        place, grads, joined, arrived, (), [(2, 4, rows, 256)], [job(1, 0), job(3, 1)], STARTS[n], rows, along_x=True
    )


def z_second_sends(place, grads, joined, arrived, got, n):
    def store(outs, value, x, z):
        for j in range(4):
            outs[0][j] = value(j)

    rows = 2 * CHUNKS[n]
    job = (2, 0, [lambda refs: refs[0].at[1]], store)
    return sums_kernel(place, grads, joined, arrived, (got,), [(4, rows, 256)], [job], STARTS[n], rows, along_x=True)


def x_later_sends(place, grads, joined, arrived, got, n):
    half = CHUNKS[n]

    def store(outs, value, x, z):
        to_1, to_3, on_3, on_1, own = outs
        far = value(x ^ 2)
        to_1[1], to_3[1] = far[:half], far[half:]
        near = value(x ^ 1)
        to_1[0], on_1[...] = near[:half], near[half:]
        near = value(x ^ 3)
        on_3[...], to_3[0] = near[:half], near[half:]
        own[...] = value(x)

    extra = [lambda refs: refs[0].at[0], lambda refs: refs[1]]
    outs = [(2, half, 256)] * 2 + [(half, 256)] * 2 + [(2 * half, 256)]
    return sums_kernel(
        place, grads, joined, arrived, got, outs, [(0, 0, extra, store)], STARTS[n], 2 * half, along_x=True
    )


def after(value, *others):
    return lax.optimization_barrier((value, *others))[0]


def dot_t(a, b):
    return lax.dot_general(a, b, (((1,), (1,)), ((), ())), preferred_element_type=f32)


def dot(a, b):
    return jnp.dot(a, b, preferred_element_type=f32)


PACKED = 7 * 128


def packed_blocks():
    for i in range(3):
        pieces = []
        for r in range(4):
            part, at = divmod(128 * i + 32 * r, 96)
            pieces.append((part, slice(at, at + 32), slice(32 * r, 32 * r + 32)))
        yield i, slice(0, 128 * (i + 1)), pieces
        yield 5 - i, slice(128 * (i + 1), PACKED), pieces


def gram_packed(place, pieces):
    count = len(CHUNKS)

    def body(place, *refs):
        total = sum(len(piece) for piece in pieces)
        parts, refs = refs[:total], refs[total:]
        nesterov, sums, outs, (padded, packed, held, sems) = refs[0], refs[1], refs[2:6], refs[6:]
        reads = []
        for n in range(count):
            rows = pl.ds(STARTS[n], 2 * CHUNKS[n])
            sources = [part if slot is None else part.at[slot] for part, (_, slot) in zip(parts[3 * n : 3 * n + 3], pieces[n])]
            reads.append(begin([(source, held.at[k, rows]) for k, source in enumerate(sources)], sems.at[n]))
        padded[FW:] = jnp.zeros((PAD - FW, 256), bf16)
        for n in range(count):
            finish(reads[n])
            rows = slice(STARTS[n], STARTS[n] + 2 * CHUNKS[n])
            mean = add(*(held[k, rows] for k in range(3))) * (1 / 32)
            value = ((1 + momentum_beta) * mean).astype(bf16)
            sums[rows] = mean.astype(bf16)
            nesterov[rows] = value
            padded[rows] = value
        for j, where, places in packed_blocks():
            block = dot_t(padded[128 * j : 128 * j + 128], padded[: 128 * (j + 1)]).astype(bf16)
            for part, rows, inside in places:
                packed[part, rows, where] = block[inside]
        for k in range(4):
            outs[k][...] = packed[place[3] ^ k]

    return call(
        body, place, [part for piece in pieces for part, _ in piece], [(FW, 256)] * 2 + [(96, PACKED)] * 4,
        [
            pltpu.VMEM((PAD, 256), bf16), pltpu.VMEM((4, 96, PACKED), bf16), pltpu.VMEM((3, FW, 256), bf16),
            pltpu.SemaphoreType.DMA((count, 3)),
        ],
    )


def iterate(place, nesterov, parts):
    scale_factor = 0.2 * math.sqrt(max(D, FW))

    def body(place, nesterov, part_0, part_1, part_2, part_3, result, packed, gram, other, mixing, current, held, sems):
        parts = (part_0, part_1, part_2, part_3)
        reads = begin([(part, packed.at[place[3] ^ k]) for k, part in enumerate(parts)] + [(nesterov, held)], sems)
        current[FW:] = jnp.zeros((PAD - FW, 256), bf16)
        finish(reads)
        total = jnp.zeros((128, 128), f32)
        eye = lax.broadcasted_iota(jnp.int32, (128, 128), 0) == lax.broadcasted_iota(jnp.int32, (128, 128), 1)
        for j, where, places in packed_blocks():
            for part, rows, inside in places:
                gram[128 * j + inside.start : 128 * j + inside.stop, : 128 * (j + 1)] = packed[part, rows, where]
            total = total + jnp.where(eye, gram[128 * j : 128 * j + 128, 128 * j : 128 * j + 128].astype(f32), 0.0)
        inverse = 1.0 / (jnp.sqrt(jnp.sum(total)) + epsilon)
        squared = inverse * inverse
        for j in range(6):
            for l in range(j + 1):
                down, across = slice(128 * j, 128 * j + 128), slice(128 * l, 128 * l + 128)
                block = gram[down, across].astype(f32) * squared
                gram[down, across] = block.astype(bf16)
                if l < j:
                    gram[across, down] = block.T.astype(bf16)
        tiles = [slice(256 * n, 256 * n + 256) for n in range(3)]
        current[:FW] = (held[...].astype(f32) * inverse).astype(bf16)
        for iteration in range(ITERS):
            for t in tiles:
                mixing[t] = (coef_b * gram[t].astype(f32) + coef_c * dot(gram[t], gram[...])).astype(bf16)
            moved = [coef_a * current[t].astype(f32) + dot(mixing[t], current[...]) for t in tiles]
            if iteration == ITERS - 1:
                for n, t in enumerate(tiles):
                    rows = slice(256 * n, min(256 * n + 256, FW))
                    result[rows] = (scale_factor * moved[n]).astype(bf16)[: rows.stop - rows.start]
                break
            for n, t in enumerate(tiles):
                current[t] = moved[n].astype(bf16)
            for t in tiles:
                other[t] = dot(mixing[t], gram[...]).astype(bf16)
            for t in tiles:
                gram[t] = (
                    coef_a * coef_a * gram[t].astype(f32) + 2 * coef_a * other[t].astype(f32) + dot(other[t], mixing[...])
                ).astype(bf16)

    square = pltpu.VMEM((PAD, PAD), bf16)
    return call(
        body, place, [nesterov, *parts], [(FW, 256)],
        [
            pltpu.VMEM((4, 96, PACKED), bf16), square, square, square,
            pltpu.VMEM((PAD, 256), bf16), pltpu.VMEM((FW, 256), bf16), pltpu.SemaphoreType.DMA((5,)),
        ],
        flops=8 * 10**9,
    )[0]


def exchange(values):
    return lax.all_to_all(values, "dp", split_axis=0, concat_axis=0, tiled=True)


def window_rows(scaled, core, chip, low):
    at = jnp.arange(WINDOW)[:, None] - (44 * chip + 22 * core - low)
    move = (at == jnp.arange(22)[None, :]).astype(bf16)
    weighted = (32 * JOIN * scaled).astype(bf16)
    moved = jnp.einsum("wr,mrc->mwc", move, weighted, preferred_element_type=f32).astype(bf16)
    return moved.reshape(4, 4, 2, WINDOW, 256)


def local(grads, mantissa, exponents):
    d = lax.axis_index("dp")
    shard = lax.axis_index("shard")
    chip, core = d // 2, d % 2
    low = jnp.minimum(44 * chip // 16 * 16, FW - WINDOW)
    place = jnp.stack([chip // 4, chip % 4, core, shard % 4, low]).astype(jnp.int32)
    spread = (jnp.arange(256)[None, :] // BLK == jnp.arange(256 // BLK)[:, None]).astype(bf16)
    scales = jnp.einsum("mrb,bc->mrc", jnp.exp2(exponents.astype(f32)).astype(bf16), spread, preferred_element_type=f32)
    scaled = mantissa.astype(f32) * scales
    window = window_rows(scaled, core, chip, low)
    grads = grads[0].reshape(4, 4, 2, FW, 256)
    last_turn = [place]

    def turn(kernel, *arguments):
        result = kernel(after(place, last_turn[0]), *arguments)
        last_turn[0] = result[0]
        return result

    def along(axis, values, steps):
        return [lax.ppermute(value, "dp", axis[k]) for value, k in zip(values, steps)]

    def of_core(which):
        return lax.dynamic_index_in_dim(window, which, 2, keepdims=False)

    to_core = {n: turn(core_rows, grads, n)[0] for n in (0, 2, 1)}
    arrived = {n: lax.ppermute(to_core[n], "dp", CORE) for n in (0, 2, 1)}
    theirs = lax.ppermute(of_core(1 - core), "dp", CORE)
    common = (grads, add(of_core(core), theirs).astype(bf16))

    def z_pieces(n):
        to_1, kept = turn(z_sends, *common, arrived[n], got[n], last[n], n)
        z_got = lax.ppermute(to_1, "dp", Z[1])
        return [(kept, 0), (z_got, 0), (lax.ppermute(add(kept[1], z_got[1]).astype(bf16), "dp", Z[2]), None)]

    got, last = {}, {}
    got[0] = along(X, turn(first_sends, *common, arrived[0], 0), (1, 3))
    z_got = lax.ppermute(turn(z_first_sends, *common, arrived[2], 2)[0], "dp", Z[1])
    first = turn(first_sends, *common, arrived[1], 1)
    z_last = lax.ppermute(turn(z_second_sends, *common, arrived[2], z_got, 2)[0], "dp", Z[2])
    second = turn(second_sends, *common, arrived[0], got[0], 0)
    last[0] = along(X, second, (3, 1))
    first = lax.optimization_barrier((*first, *got[0], *second))[:2]
    got[1] = along(X, first, (1, 3))
    to_1, to_3, on_3, on_1, own = turn(x_later_sends, *common, arrived[2], (z_got, z_last), 2)
    pieces = [z_pieces(0)]
    last[1] = along(X, turn(second_sends, *common, arrived[1], got[1], 1), (3, 1))
    got_1, got_3 = along(X, lax.optimization_barrier((to_1, to_3, *got[1]))[:2], (1, 3))
    on_3, on_1 = add(on_3, got_1[1]).astype(bf16), add(on_1, got_3[1]).astype(bf16)
    on_3, on_1 = along(X, (on_3, on_1), (3, 1))
    last_turn[0] = after(last_turn[0], pieces[0][1][0])
    pieces.append(z_pieces(1))
    received = jnp.concatenate([got_1[0], got_3[0]], axis=0), jnp.concatenate([on_3, on_1], axis=0)
    pieces.append([(own, None), (received[0], None), (received[1], None)])
    nesterov, sums, mine, *others = gram_packed(place, pieces)
    mine = add(mine, *(lax.ppermute(other, "shard", Y[k]) for k, other in zip((1, 2, 3), others))).astype(bf16)
    mine = add(mine, lax.ppermute(mine, "shard", Y[4])).astype(bf16)
    parts = [mine] + [lax.ppermute(mine, "shard", Y[k]) for k in (1, 2, 3)]
    update = iterate(place, nesterov, parts)
    both = exchange(jnp.concatenate([update.reshape(32, 22, 256), sums.reshape(32, 22, 256)], axis=1))
    return (both[:, :22], (momentum_beta - JOIN) * scaled + both[:, 22:].astype(f32))


def solution(mesh):
    in_specs = (P("dp", None, None, "shard"), P(None, "dp", "shard"), P(None, "dp", "shard"))
    out_specs = (P(None, "dp", "shard"), P(None, "dp", "shard"))
    return jax.shard_map(local, mesh=mesh, in_specs=in_specs, out_specs=out_specs, check_vma=False)
```

```python
import math

import jax
import jax.numpy as jnp
from jax import lax
from jax.experimental import pallas as pl
from jax.experimental.pallas import tpu as pltpu
from jax.sharding import PartitionSpec as P

D = 2048
FW = 704
BLK = 32
ITERS = 3

coef_a = 3.4445
coef_b = -4.775
coef_c = 2.0315
momentum_beta = 0.95
epsilon = 1e-07
bf16 = jnp.bfloat16
f32 = jnp.float32

CHUNKS = (144,112,96)
STARTS = [2 * sum(CHUNKS[:n]) for n in range(len(CHUNKS))]
PAD = 768
JOIN = momentum_beta * momentum_beta / (1 + momentum_beta)
WINDOW = 64


def dp_moves(move):
    pairs = []
    for x in range(4):
        for z in range(4):
            for core in range(2):
                nx, nz, nc = move(x, z, core)
                pairs.append((x * 8 + z * 2 + core, nx * 8 + nz * 2 + nc))
    return pairs


CORE = dp_moves(lambda x, z, core: (x, z, 1 - core))
X = {k: dp_moves(lambda x, z, core, k=k: (x ^ k, z, core)) for k in (1, 3)}
Z = {k: dp_moves(lambda x, z, core, k=k: (x, z ^ k, core)) for k in (1, 2)}
Y = {k: [(s, s ^ k) for s in range(8)] for k in (1, 2, 3, 4)}


def add(*terms):
    total = terms[0].astype(f32)
    for term in terms[1:]:
        total = total + term.astype(f32)
    return total


LARGE = 50 * 2**20
VMEM = 14 * 2**20


TOKEN = jax.ShapeDtypeStruct((16, 128), bf16)


def call(body, place, operands, outs, scratch, flops=0, vmem=VMEM, space=pltpu.VMEM):
    place, *waited = place
    first = 1 + len(operands)

    def with_token(*refs):
        rest = refs[first + len(waited) :]
        token = rest[len(outs)]
        token[...] = jnp.zeros_like(token)
        body(*refs[:first], *rest[: len(outs)], *rest[len(outs) + 1 :])

    return pl.pallas_call(
        with_token,
        out_shape=[jax.ShapeDtypeStruct(shape, bf16) for shape in outs] + [TOKEN],
        in_specs=[pl.BlockSpec(memory_space=pltpu.SMEM)] + [pl.BlockSpec(memory_space=pl.ANY)] * (first - 1 + len(waited)),
        out_specs=[pl.BlockSpec(memory_space=space)] * len(outs) + [pl.BlockSpec(memory_space=pltpu.VMEM)],
        scratch_shapes=scratch,
        compiler_params=pltpu.CompilerParams(vmem_limit_bytes=vmem),
        cost_estimate=pl.CostEstimate(flops=flops, bytes_accessed=6000000, transcendentals=0),
    )(place, *operands, *waited)


def begin(pairs, sems):
    copies = [pltpu.make_async_copy(source, target, sems.at[n]) for n, (source, target) in enumerate(pairs)]
    for copy in copies:
        copy.start()
    return copies


def finish(copies):
    for copy in copies:
        copy.wait()


def core_rows(place, grads, chunks):
    def body(place, grads, *refs):
        outs, buffers, (sems, out_sems) = refs[: len(chunks)], refs[len(chunks) : -2], refs[-2:]
        pairs, targets = [], []
        for n, out, buffer in zip(chunks, outs, buffers):
            rows = pl.ds(STARTS[n], 2 * CHUNKS[n])
            for x in range(4):
                pairs.append((grads.at[x, :, 1 - place[2], rows], buffer.at[x]))
                targets.append((buffer.at[x], out.at[x]))
        writes = []
        for n, read in enumerate(begin(pairs, sems)):
            read.wait()
            writes.append(pltpu.make_async_copy(*targets[n], out_sems.at[n]))
            writes[n].start()
        finish(writes)

    shapes = [(4, 4, 2 * CHUNKS[n], 256) for n in chunks]
    sems = [pltpu.SemaphoreType.DMA((4 * len(chunks),))] * 2
    return call(
        body, place, (grads,), shapes, [pltpu.VMEM(shape, bf16) for shape in shapes] + sems, vmem=LARGE, space=pl.ANY
    )


def tree_add(terms):
    while len(terms) > 1:
        terms = [sum(terms[n + 1 : n + 2], terms[n]) for n in range(0, len(terms), 2)]
    return terms[0]


def sums_kernel(place, grads, joined, arrived, others, outs, jobs, start, rows, along_x=False):
    count = len(jobs)
    terms = 2 + max(len(job[2]) for job in jobs)

    def body(place, grads, joined, arrived, *refs):
        others_in, refs = refs[: len(others)], refs[len(others) :]
        outs_ref, (buffers, window, sems) = refs[: len(outs)], refs[len(outs) :]
        x, z, core = place[0], place[1], place[2]
        reads = []
        for n, (k, first, extra, _) in enumerate(jobs):
            which = (slice(None), z ^ k) if along_x else (x ^ k, slice(None))
            pairs = [
                (grads.at[(*which, core, pl.ds(start + first, rows))], buffers.at[n, 0]),
                (joined.at[which], window.at[n]),
                (arrived.at[(*which, pl.ds(first, rows))], buffers.at[n, 1]),
            ]
            pairs += [(term(others_in), buffers.at[n, 2 + t]) for t, term in enumerate(extra)]
            reads.append(begin(pairs, sems.at[n]))
        for n, (k, first, extra, store) in enumerate(jobs):
            finish(reads[n])
            for i in range(WINDOW // 16):
                at = place[4] + 16 * i - start - first

                @pl.when((at >= 0) & (at < rows))
                def _(n=n, i=i, at=at):
                    there = pl.ds(pl.multiple_of(at, 16), 16)
                    buffers[n, 0, :, there] = add(buffers[n, 0, :, there], window[n, :, 16 * i : 16 * i + 16]).astype(bf16)

            store(outs_ref, lambda j: tree_add([buffers[n, t, j] for t in range(2 + len(extra))]), x, z)

    return call(
        body, place, (grads, joined, arrived, *others), outs,
        [
            pltpu.VMEM((count, terms, 4, rows, 256), bf16),
            pltpu.VMEM((count, 4, WINDOW, 256), bf16),
            pltpu.SemaphoreType.DMA((count, terms + 1)),
        ],
        vmem=LARGE,
    )


def first_sends(place, grads, joined, arrived, n):
    half = CHUNKS[n]

    def job(k, part, slot):
        def store(outs, value, x, z):
            for j in range(4):
                outs[part][slot, j] = value(j)

        return (k, part * half, [], store)

    jobs = [job(2, 0, 1), job(1, 0, 0), job(2, 1, 1), job(3, 1, 0)]
    return sums_kernel(place, grads, joined, arrived, (), [(2, 4, half, 256)] * 2, jobs, STARTS[n], half)


def second_sends(place, grads, joined, arrived, got, n):
    half = CHUNKS[n]

    def job(k, part):
        def store(outs, value, x, z):
            for j in range(4):
                outs[part][j] = value(j)

        return (k, part * half, [lambda refs: refs[part].at[1]], store)

    return sums_kernel(
        place, grads, joined, arrived, got, [(4, half, 256)] * 2, [job(3, 0), job(1, 1)], STARTS[n], half
    )


def z_sends(place, grads, joined, arrived, got, last, n):
    half = CHUNKS[n]

    def job(part):
        def store(outs, value, x, z):
            rows = slice(part * half, part * half + half)
            for out, slot, k in ((0, 0, 1), (0, 1, 3), (1, 0, 0), (1, 1, 2)):
                outs[out][slot, rows] = value(z ^ k)

        return (0, part * half, [lambda refs: refs[part].at[0], lambda refs: refs[2 + part]], store)

    return sums_kernel(
        place, grads, joined, arrived, (*got, *last), [(2, 2 * half, 256)] * 2, [job(0), job(1)], STARTS[n], half
    )


def z_first_sends(place, grads, joined, arrived, n):
    def job(k, slot):
        def store(outs, value, x, z):
            for j in range(4):
                outs[0][slot, j] = value(j)

        return (k, 0, [], store)

    rows = 2 * CHUNKS[n]
    return sums_kernel(
        place, grads, joined, arrived, (), [(2, 4, rows, 256)], [job(1, 0), job(3, 1)], STARTS[n], rows, along_x=True
    )


def z_second_sends(place, grads, joined, arrived, got, n):
    def store(outs, value, x, z):
        for j in range(4):
            outs[0][j] = value(j)

    rows = 2 * CHUNKS[n]
    job = (2, 0, [lambda refs: refs[0].at[1]], store)
    return sums_kernel(place, grads, joined, arrived, (got,), [(4, rows, 256)], [job], STARTS[n], rows, along_x=True)


def x_later_sends(place, grads, joined, arrived, got, n):
    half = CHUNKS[n]

    def store(outs, value, x, z):
        to_1, to_3, on_3, on_1, own = outs
        far = value(x ^ 2)
        to_1[1], to_3[1] = far[:half], far[half:]
        near = value(x ^ 1)
        to_1[0], on_1[...] = near[:half], near[half:]
        near = value(x ^ 3)
        on_3[...], to_3[0] = near[:half], near[half:]
        own[...] = value(x)

    extra = [lambda refs: refs[0].at[0], lambda refs: refs[1]]
    outs = [(2, half, 256)] * 2 + [(half, 256)] * 2 + [(2 * half, 256)]
    return sums_kernel(
        place, grads, joined, arrived, got, outs, [(0, 0, extra, store)], STARTS[n], 2 * half, along_x=True
    )


def dot_t(a, b):
    return lax.dot_general(a, b, (((1,), (1,)), ((), ())), preferred_element_type=f32)


def dot(a, b):
    return jnp.dot(a, b, preferred_element_type=f32)


PACKED = 7 * 128


def packed_blocks():
    for i in range(3):
        pieces = []
        for r in range(4):
            part, at = divmod(128 * i + 32 * r, 96)
            pieces.append((part, slice(at, at + 32), slice(32 * r, 32 * r + 32)))
        yield i, slice(0, 128 * (i + 1)), pieces
        yield 5 - i, slice(128 * (i + 1), PACKED), pieces


def gram_packed(place, pieces):
    count = len(CHUNKS)

    def body(place, *refs):
        total = sum(len(piece) for piece in pieces)
        parts, refs = refs[:total], refs[total:]
        nesterov, sums, outs, (padded, packed, held, sems) = refs[0], refs[1], refs[2:6], refs[6:]
        reads = []
        for n in range(count):
            rows = pl.ds(STARTS[n], 2 * CHUNKS[n])
            sources = [part if slot is None else part.at[slot] for part, (_, slot) in zip(parts[3 * n : 3 * n + 3], pieces[n])]
            reads.append(begin([(source, held.at[k, rows]) for k, source in enumerate(sources)], sems.at[n]))
        padded[FW:] = jnp.zeros((PAD - FW, 256), bf16)
        for n in range(count):
            finish(reads[n])
            rows = slice(STARTS[n], STARTS[n] + 2 * CHUNKS[n])
            mean = add(*(held[k, rows] for k in range(3))) * (1 / 32)
            value = ((1 + momentum_beta) * mean).astype(bf16)
            sums[rows] = mean.astype(bf16)
            nesterov[rows] = value
            padded[rows] = value
        for j, where, places in packed_blocks():
            block = dot_t(padded[128 * j : 128 * j + 128], padded[: 128 * (j + 1)]).astype(bf16)
            for part, rows, inside in places:
                packed[part, rows, where] = block[inside]
        for k in range(4):
            outs[k][...] = packed[place[3] ^ k]

    return call(
        body, place, [part for piece in pieces for part, _ in piece], [(FW, 256)] * 2 + [(96, PACKED)] * 4,
        [
            pltpu.VMEM((PAD, 256), bf16), pltpu.VMEM((4, 96, PACKED), bf16), pltpu.VMEM((3, FW, 256), bf16),
            pltpu.SemaphoreType.DMA((count, 3)),
        ],
    )


def iterate(place, nesterov, parts):
    scale_factor = 0.2 * math.sqrt(max(D, FW))

    def body(place, nesterov, part_0, part_1, part_2, part_3, result, packed, gram, other, mixing, current, applied, held, sems):
        parts = (part_0, part_1, part_2, part_3)
        reads = begin([(part, packed.at[place[3] ^ k]) for k, part in enumerate(parts)] + [(nesterov, held)], sems)
        current[FW:] = jnp.zeros((PAD - FW, 256), bf16)
        finish(reads)
        total = jnp.zeros((128, 128), f32)
        eye = lax.broadcasted_iota(jnp.int32, (128, 128), 0) == lax.broadcasted_iota(jnp.int32, (128, 128), 1)
        for j, where, places in packed_blocks():
            for part, rows, inside in places:
                gram[128 * j + inside.start : 128 * j + inside.stop, : 128 * (j + 1)] = packed[part, rows, where]
            total = total + jnp.where(eye, gram[128 * j : 128 * j + 128, 128 * j : 128 * j + 128].astype(f32), 0.0)
        inverse = 1.0 / (jnp.sqrt(jnp.sum(total)) + epsilon)
        squared = inverse * inverse
        for j in range(6):
            for l in range(j + 1):
                down, across = slice(128 * j, 128 * j + 128), slice(128 * l, 128 * l + 128)
                block = gram[down, across].astype(f32) * squared
                gram[down, across] = block.astype(bf16)
                if l < j:
                    gram[across, down] = block.T.astype(bf16)
        tiles = [slice(256 * n, 256 * n + 256) for n in range(3)]
        current[:FW] = (held[...].astype(f32) * inverse).astype(bf16)
        for iteration in range(ITERS):
            if iteration == ITERS - 1:
                for t in tiles:
                    applied[t] = dot(gram[t], current[...]).astype(bf16)
                for n, t in enumerate(tiles):
                    value = coef_a * current[t].astype(f32) + coef_b * applied[t].astype(f32)
                    value = scale_factor * (value + coef_c * dot(gram[t], applied[...]))
                    rows = slice(256 * n, min(256 * n + 256, FW))
                    result[rows] = value.astype(bf16)[: rows.stop - rows.start]
                break
            for t in tiles:
                mixing[t] = (coef_b * gram[t].astype(f32) + coef_c * dot(gram[t], gram[...])).astype(bf16)
            moved = [coef_a * current[t].astype(f32) + dot(mixing[t], current[...]) for t in tiles]
            for n, t in enumerate(tiles):
                current[t] = moved[n].astype(bf16)
            for t in tiles:
                other[t] = dot(mixing[t], gram[...]).astype(bf16)
            for t in tiles:
                gram[t] = (
                    coef_a * coef_a * gram[t].astype(f32) + 2 * coef_a * other[t].astype(f32) + dot(other[t], mixing[...])
                ).astype(bf16)

    square = pltpu.VMEM((PAD, PAD), bf16)
    return call(
        body, place, [nesterov, *parts], [(FW, 256)],
        [
            pltpu.VMEM((4, 96, PACKED), bf16), square, square, square,
            pltpu.VMEM((PAD, 256), bf16), pltpu.VMEM((PAD, 256), bf16), pltpu.VMEM((FW, 256), bf16),
            pltpu.SemaphoreType.DMA((5,)),
        ],
        flops=8 * 10**9,
    )


def exchange(values):
    return lax.all_to_all(values, "dp", split_axis=0, concat_axis=0, tiled=True)


def window_rows(scaled, core, chip, low):
    at = jnp.arange(WINDOW)[:, None] - (44 * chip + 22 * core - low)
    move = (at == jnp.arange(22)[None, :]).astype(bf16)
    weighted = (32 * JOIN * scaled).astype(bf16)
    moved = jnp.einsum("wr,mrc->mwc", move, weighted, preferred_element_type=f32).astype(bf16)
    return moved.reshape(4, 4, 2, WINDOW, 256)


def local(grads, mantissa, exponents):
    d = lax.axis_index("dp")
    shard = lax.axis_index("shard")
    chip, core = d // 2, d % 2
    low = jnp.minimum(44 * chip // 16 * 16, FW - WINDOW)
    place = jnp.stack([chip // 4, chip % 4, core, shard % 4, low]).astype(jnp.int32)
    spread = (jnp.arange(256)[None, :] // BLK == jnp.arange(256 // BLK)[:, None]).astype(bf16)
    scales = jnp.einsum("mrb,bc->mrc", jnp.exp2(exponents.astype(f32)).astype(bf16), spread, preferred_element_type=f32)
    scaled = mantissa.astype(f32) * scales
    window = window_rows(scaled, core, chip, low)
    grads = grads[0].reshape(4, 4, 2, FW, 256)
    token = []

    def turn(kernel, *arguments, waited=()):
        *results, last = kernel([place, *token, *waited], *arguments)
        token[:] = [last]
        return results

    def along(axis, values, steps):
        return [lax.ppermute(value, "dp", axis[k]) for value, k in zip(values, steps)]

    def of_core(which):
        return lax.dynamic_index_in_dim(window, which, 2, keepdims=False)

    def z_start(n):
        to_1, kept = turn(z_sends, *common, arrived[n], got[n], last[n], n)
        return kept, lax.ppermute(to_1, "dp", Z[1])

    def z_end(kept, z_got):
        return [(kept, 0), (z_got, 0), (lax.ppermute(add(kept[1], z_got[1]).astype(bf16), "dp", Z[2]), None)]

    arrived, got, last = {}, {}, {}
    to_core = turn(core_rows, grads, (0, 2))
    arrived[0], arrived[2] = along({0: CORE}, to_core, (0, 0))
    theirs = lax.ppermute(of_core(1 - core), "dp", CORE)
    common = (grads, add(of_core(core), theirs).astype(bf16))
    arrived[1] = lax.ppermute(turn(core_rows, grads, (1,), waited=(theirs, arrived[2]))[0], "dp", CORE)
    got[0] = along(X, turn(first_sends, *common, arrived[0], 0), (1, 3))
    b_got = lax.ppermute(turn(z_first_sends, *common, arrived[2], 2)[0], "dp", Z[1])
    first = turn(first_sends, *common, arrived[1], 1)
    b_last = lax.ppermute(turn(z_second_sends, *common, arrived[2], b_got, 2)[0], "dp", Z[2])
    second = turn(second_sends, *common, arrived[0], got[0], 0)
    last[0] = along(X, second, (3, 1))
    got[1] = along(X, first, (1, 3))
    last[1] = along(X, turn(second_sends, *common, arrived[1], got[1], 1), (3, 1))
    pieces = [z_end(*z_start(0)), z_end(*z_start(1))]
    to_1, to_3, on_3, on_1, own = turn(x_later_sends, *common, arrived[2], (b_got, b_last), 2)
    got_1, got_3 = along(X, (to_1, to_3), (1, 3))
    on_3, on_1 = add(on_3, got_1[1]).astype(bf16), add(on_1, got_3[1]).astype(bf16)
    on_3, on_1 = along(X, (on_3, on_1), (3, 1))
    received = jnp.concatenate([got_1[0], got_3[0]], axis=0), jnp.concatenate([on_3, on_1], axis=0)
    pieces.append([(own, None), (received[0], None), (received[1], None)])
    nesterov, sums, mine, *others = turn(gram_packed, pieces)
    mine = add(mine, *(lax.ppermute(other, "shard", Y[k]) for k, other in zip((1, 2, 3), others))).astype(bf16)
    mine = add(mine, lax.ppermute(mine, "shard", Y[4])).astype(bf16)
    parts = [mine] + [lax.ppermute(mine, "shard", Y[k]) for k in (1, 2, 3)]
    update = turn(iterate, nesterov, parts)[0]
    both = exchange(jnp.concatenate([update.reshape(32, 22, 256), sums.reshape(32, 22, 256)], axis=1))
    return (both[:, :22], (momentum_beta - JOIN) * scaled + both[:, 22:].astype(f32))


def solution(mesh):
    in_specs = (P("dp", None, None, "shard"), P(None, "dp", "shard"), P(None, "dp", "shard"))
    out_specs = (P(None, "dp", "shard"), P(None, "dp", "shard"))
    return jax.shard_map(local, mesh=mesh, in_specs=in_specs, out_specs=out_specs, check_vma=False)
```

```python
import math

import jax
import jax.numpy as jnp
from jax import lax
from jax.experimental import pallas as pl
from jax.experimental.pallas import tpu as pltpu
from jax.sharding import PartitionSpec as P

D = 2048
FW = 704
BLK = 32
ITERS = 3

coef_a = 3.4445
coef_b = -4.775
coef_c = 2.0315
momentum_beta = 0.95
epsilon = 1e-07
bf16 = jnp.bfloat16
f32 = jnp.float32

CHUNKS = (144,112,96)
STARTS = [2 * sum(CHUNKS[:n]) for n in range(len(CHUNKS))]
PAD = 768
JOIN = momentum_beta * momentum_beta / (1 + momentum_beta)
WINDOW = 64


def dp_moves(move):
    pairs = []
    for x in range(4):
        for z in range(4):
            for core in range(2):
                nx, nz, nc = move(x, z, core)
                pairs.append((x * 8 + z * 2 + core, nx * 8 + nz * 2 + nc))
    return pairs


CORE = dp_moves(lambda x, z, core: (x, z, 1 - core))
X = {k: dp_moves(lambda x, z, core, k=k: (x ^ k, z, core)) for k in (1, 3)}
Z = {k: dp_moves(lambda x, z, core, k=k: (x, z ^ k, core)) for k in (1, 2)}
Y = {k: [(s, s ^ k) for s in range(8)] for k in (1, 2, 3, 4)}


def add(*terms):
    total = terms[0].astype(f32)
    for term in terms[1:]:
        total = total + term.astype(f32)
    return total


LARGE = 50 * 2**20
VMEM = 14 * 2**20


TOKEN = jax.ShapeDtypeStruct((16, 128), bf16)


def call(body, place, operands, outs, scratch, flops=0, vmem=VMEM, space=pltpu.VMEM):
    place, *waited = place
    first = 1 + len(operands)

    def with_token(*refs):
        rest = refs[first + len(waited) :]
        token = rest[len(outs)]
        token[...] = jnp.zeros_like(token)
        body(*refs[:first], *rest[: len(outs)], *rest[len(outs) + 1 :])

    return pl.pallas_call(
        with_token,
        out_shape=[jax.ShapeDtypeStruct(shape, bf16) for shape in outs] + [TOKEN],
        in_specs=[pl.BlockSpec(memory_space=pltpu.SMEM)] + [pl.BlockSpec(memory_space=pl.ANY)] * (first - 1 + len(waited)),
        out_specs=[pl.BlockSpec(memory_space=space)] * len(outs) + [pl.BlockSpec(memory_space=pltpu.VMEM)],
        scratch_shapes=scratch,
        compiler_params=pltpu.CompilerParams(vmem_limit_bytes=vmem),
        cost_estimate=pl.CostEstimate(flops=flops, bytes_accessed=6000000, transcendentals=0),
    )(place, *operands, *waited)


def begin(pairs, sems):
    copies = [pltpu.make_async_copy(source, target, sems.at[n]) for n, (source, target) in enumerate(pairs)]
    for copy in copies:
        copy.start()
    return copies


def finish(copies):
    for copy in copies:
        copy.wait()


def core_rows(place, grads, chunks):
    def body(place, grads, *refs):
        outs, buffers, (sems, out_sems) = refs[: len(chunks)], refs[len(chunks) : -2], refs[-2:]
        pairs, targets = [], []
        for n, out, buffer in zip(chunks, outs, buffers):
            rows = pl.ds(STARTS[n], 2 * CHUNKS[n])
            for x in range(4):
                pairs.append((grads.at[x, :, 1 - place[2], rows], buffer.at[x]))
                targets.append((buffer.at[x], out.at[x]))
        writes = []
        for n, read in enumerate(begin(pairs, sems)):
            read.wait()
            writes.append(pltpu.make_async_copy(*targets[n], out_sems.at[n]))
            writes[n].start()
        finish(writes)

    shapes = [(4, 4, 2 * CHUNKS[n], 256) for n in chunks]
    sems = [pltpu.SemaphoreType.DMA((4 * len(chunks),))] * 2
    return call(
        body, place, (grads,), shapes, [pltpu.VMEM(shape, bf16) for shape in shapes] + sems, vmem=LARGE, space=pl.ANY
    )


def tree_add(terms):
    while len(terms) > 1:
        terms = [sum(terms[n + 1 : n + 2], terms[n]) for n in range(0, len(terms), 2)]
    return terms[0]


def sums_kernel(place, grads, joined, arrived, others, outs, jobs, start, rows, along_x=False):
    count = len(jobs)
    terms = 2 + max(len(job[2]) for job in jobs)

    def body(place, grads, joined, arrived, *refs):
        others_in, refs = refs[: len(others)], refs[len(others) :]
        outs_ref, (buffers, window, sems) = refs[: len(outs)], refs[len(outs) :]
        x, z, core = place[0], place[1], place[2]
        reads = []
        for n, (k, first, extra, _) in enumerate(jobs):
            which = (slice(None), z ^ k) if along_x else (x ^ k, slice(None))
            pairs = [
                (grads.at[(*which, core, pl.ds(start + first, rows))], buffers.at[n, 0]),
                (joined.at[which], window.at[n]),
                (arrived.at[(*which, pl.ds(first, rows))], buffers.at[n, 1]),
            ]
            pairs += [(term(others_in), buffers.at[n, 2 + t]) for t, term in enumerate(extra)]
            reads.append(begin(pairs, sems.at[n]))
        for n, (k, first, extra, store) in enumerate(jobs):
            finish(reads[n])
            for i in range(WINDOW // 16):
                at = place[4] + 16 * i - start - first

                @pl.when((at >= 0) & (at < rows))
                def _(n=n, i=i, at=at):
                    there = pl.ds(pl.multiple_of(at, 16), 16)
                    buffers[n, 0, :, there] = add(buffers[n, 0, :, there], window[n, :, 16 * i : 16 * i + 16]).astype(bf16)

            store(outs_ref, lambda j: tree_add([buffers[n, t, j] for t in range(2 + len(extra))]), x, z)

    return call(
        body, place, (grads, joined, arrived, *others), outs,
        [
            pltpu.VMEM((count, terms, 4, rows, 256), bf16),
            pltpu.VMEM((count, 4, WINDOW, 256), bf16),
            pltpu.SemaphoreType.DMA((count, terms + 1)),
        ],
        vmem=LARGE,
    )


def first_sends(place, grads, joined, arrived, n):
    half = CHUNKS[n]

    def job(k, part, slot):
        def store(outs, value, x, z):
            for j in range(4):
                outs[part][slot, j] = value(j)

        return (k, part * half, [], store)

    jobs = [job(2, 0, 1), job(1, 0, 0), job(2, 1, 1), job(3, 1, 0)]
    return sums_kernel(place, grads, joined, arrived, (), [(2, 4, half, 256)] * 2, jobs, STARTS[n], half)


def second_sends(place, grads, joined, arrived, got, n):
    half = CHUNKS[n]

    def job(k, part):
        def store(outs, value, x, z):
            for j in range(4):
                outs[part][j] = value(j)

        return (k, part * half, [lambda refs: refs[part].at[1]], store)

    return sums_kernel(
        place, grads, joined, arrived, got, [(4, half, 256)] * 2, [job(3, 0), job(1, 1)], STARTS[n], half
    )


def z_sends(place, grads, joined, arrived, got, last, n):
    half = CHUNKS[n]

    def job(part):
        def store(outs, value, x, z):
            rows = slice(part * half, part * half + half)
            for out, slot, k in ((0, 0, 1), (0, 1, 3), (1, 0, 0), (1, 1, 2)):
                outs[out][slot, rows] = value(z ^ k)

        return (0, part * half, [lambda refs: refs[part].at[0], lambda refs: refs[2 + part]], store)

    return sums_kernel(
        place, grads, joined, arrived, (*got, *last), [(2, 2 * half, 256)] * 2, [job(0), job(1)], STARTS[n], half
    )


def z_first_sends(place, grads, joined, arrived, n):
    def job(k, slot):
        def store(outs, value, x, z):
            for j in range(4):
                outs[0][slot, j] = value(j)

        return (k, 0, [], store)

    rows = 2 * CHUNKS[n]
    return sums_kernel(
        place, grads, joined, arrived, (), [(2, 4, rows, 256)], [job(1, 0), job(3, 1)], STARTS[n], rows, along_x=True
    )


def z_second_sends(place, grads, joined, arrived, got, n):
    def store(outs, value, x, z):
        for j in range(4):
            outs[0][j] = value(j)

    rows = 2 * CHUNKS[n]
    job = (2, 0, [lambda refs: refs[0].at[1]], store)
    return sums_kernel(place, grads, joined, arrived, (got,), [(4, rows, 256)], [job], STARTS[n], rows, along_x=True)


def x_later_sends(place, grads, joined, arrived, got, n):
    half = CHUNKS[n]

    def store(outs, value, x, z):
        to_1, to_3, on_3, on_1, own = outs
        far = value(x ^ 2)
        to_1[1], to_3[1] = far[:half], far[half:]
        near = value(x ^ 1)
        to_1[0], on_1[...] = near[:half], near[half:]
        near = value(x ^ 3)
        on_3[...], to_3[0] = near[:half], near[half:]
        own[...] = value(x)

    extra = [lambda refs: refs[0].at[0], lambda refs: refs[1]]
    outs = [(2, half, 256)] * 2 + [(half, 256)] * 2 + [(2 * half, 256)]
    return sums_kernel(
        place, grads, joined, arrived, got, outs, [(0, 0, extra, store)], STARTS[n], 2 * half, along_x=True
    )


def dot_t(a, b):
    return lax.dot_general(a, b, (((1,), (1,)), ((), ())), preferred_element_type=f32)


def dot(a, b):
    return jnp.dot(a, b, preferred_element_type=f32)


PACKED = 7 * 128


def packed_blocks():
    for i in range(3):
        pieces = []
        for r in range(4):
            part, at = divmod(128 * i + 32 * r, 96)
            pieces.append((part, slice(at, at + 32), slice(32 * r, 32 * r + 32)))
        yield i, slice(0, 128 * (i + 1)), pieces
        yield 5 - i, slice(128 * (i + 1), PACKED), pieces


def gram_packed(place, pieces):
    count = len(CHUNKS)

    def body(place, *refs):
        total = sum(len(piece) for piece in pieces)
        parts, refs = refs[:total], refs[total:]
        nesterov, sums, outs, (padded, packed, held, sems) = refs[0], refs[1], refs[2:6], refs[6:]
        reads = []
        for n in range(count):
            rows = pl.ds(STARTS[n], 2 * CHUNKS[n])
            sources = [part if slot is None else part.at[slot] for part, (_, slot) in zip(parts[3 * n : 3 * n + 3], pieces[n])]
            reads.append(begin([(source, held.at[k, rows]) for k, source in enumerate(sources)], sems.at[n]))
        padded[FW:] = jnp.zeros((PAD - FW, 256), bf16)
        for n in range(count):
            finish(reads[n])
            rows = slice(STARTS[n], STARTS[n] + 2 * CHUNKS[n])
            mean = add(*(held[k, rows] for k in range(3))) * (1 / 32)
            value = ((1 + momentum_beta) * mean).astype(bf16)
            sums[rows] = mean.astype(bf16)
            nesterov[rows] = value
            padded[rows] = value
        for j, where, places in packed_blocks():
            block = dot_t(padded[128 * j : 128 * j + 128], padded[: 128 * (j + 1)]).astype(bf16)
            for part, rows, inside in places:
                packed[part, rows, where] = block[inside]
        for k in range(4):
            outs[k][...] = packed[place[3] ^ k]

    return call(
        body, place, [part for piece in pieces for part, _ in piece], [(FW, 256)] * 2 + [(96, PACKED)] * 4,
        [
            pltpu.VMEM((PAD, 256), bf16), pltpu.VMEM((4, 96, PACKED), bf16), pltpu.VMEM((3, FW, 256), bf16),
            pltpu.SemaphoreType.DMA((count, 3)),
        ],
    )


def iterate(place, nesterov, parts):
    scale_factor = 0.2 * math.sqrt(max(D, FW))

    def body(place, nesterov, part_0, part_1, part_2, part_3, result, packed, gram, other, mixing, current, applied, held, sems):
        parts = (part_0, part_1, part_2, part_3)
        reads = begin([(part, packed.at[place[3] ^ k]) for k, part in enumerate(parts)] + [(nesterov, held)], sems)
        current[FW:] = jnp.zeros((PAD - FW, 256), bf16)
        finish(reads)
        total = jnp.zeros((128, 128), f32)
        eye = lax.broadcasted_iota(jnp.int32, (128, 128), 0) == lax.broadcasted_iota(jnp.int32, (128, 128), 1)
        for j, where, places in packed_blocks():
            for part, rows, inside in places:
                gram[128 * j + inside.start : 128 * j + inside.stop, : 128 * (j + 1)] = packed[part, rows, where]
            total = total + jnp.where(eye, gram[128 * j : 128 * j + 128, 128 * j : 128 * j + 128].astype(f32), 0.0)
        inverse = 1.0 / (jnp.sqrt(jnp.sum(total)) + epsilon)
        squared = inverse * inverse
        for j in range(6):
            for l in range(j + 1):
                down, across = slice(128 * j, 128 * j + 128), slice(128 * l, 128 * l + 128)
                block = gram[down, across].astype(f32) * squared
                gram[down, across] = block.astype(bf16)
                if l < j:
                    gram[across, down] = block.T.astype(bf16)
        tiles = [slice(256 * n, 256 * n + 256) for n in range(3)]
        current[:FW] = (held[...].astype(f32) * inverse).astype(bf16)
        for iteration in range(ITERS):
            if iteration == ITERS - 1:
                for t in tiles:
                    applied[t] = dot(gram[t], current[...]).astype(bf16)
                for n, t in enumerate(tiles):
                    value = coef_a * current[t].astype(f32) + coef_b * applied[t].astype(f32)
                    value = scale_factor * (value + coef_c * dot(gram[t], applied[...]))
                    rows = slice(256 * n, min(256 * n + 256, FW))
                    result[rows] = value.astype(bf16)[: rows.stop - rows.start]
                break
            for t in tiles:
                mixing[t] = (coef_b * gram[t].astype(f32) + coef_c * dot(gram[t], gram[...])).astype(bf16)
            moved = [coef_a * current[t].astype(f32) + dot(mixing[t], current[...]) for t in tiles]
            for n, t in enumerate(tiles):
                current[t] = moved[n].astype(bf16)
            for t in tiles:
                other[t] = dot(mixing[t], gram[...]).astype(bf16)
            for t in tiles:
                gram[t] = (
                    coef_a * coef_a * gram[t].astype(f32) + 2 * coef_a * other[t].astype(f32) + dot(other[t], mixing[...])
                ).astype(bf16)

    square = pltpu.VMEM((PAD, PAD), bf16)
    return call(
        body, place, [nesterov, *parts], [(FW, 256)],
        [
            pltpu.VMEM((4, 96, PACKED), bf16), square, square, square,
            pltpu.VMEM((PAD, 256), bf16), pltpu.VMEM((PAD, 256), bf16), pltpu.VMEM((FW, 256), bf16),
            pltpu.SemaphoreType.DMA((5,)),
        ],
        flops=8 * 10**9,
    )


def exchange(values):
    return lax.all_to_all(values, "dp", split_axis=0, concat_axis=0, tiled=True)


def window_rows(scaled, core, chip, low):
    at = jnp.arange(WINDOW)[:, None] - (44 * chip + 22 * core - low)
    move = (at == jnp.arange(22)[None, :]).astype(bf16)
    weighted = (32 * JOIN * scaled).astype(bf16)
    moved = jnp.einsum("wr,mrc->mwc", move, weighted, preferred_element_type=f32).astype(bf16)
    return moved.reshape(4, 4, 2, WINDOW, 256)


def local(grads, mantissa, exponents):
    d = lax.axis_index("dp")
    shard = lax.axis_index("shard")
    chip, core = d // 2, d % 2
    low = jnp.minimum(44 * chip // 16 * 16, FW - WINDOW)
    place = jnp.stack([chip // 4, chip % 4, core, shard % 4, low]).astype(jnp.int32)
    spread = (jnp.arange(256)[None, :] // BLK == jnp.arange(256 // BLK)[:, None]).astype(bf16)
    scales = jnp.einsum("mrb,bc->mrc", jnp.exp2(exponents.astype(f32)).astype(bf16), spread, preferred_element_type=f32)
    scaled = mantissa.astype(f32) * scales
    window = window_rows(scaled, core, chip, low)
    grads = grads[0].reshape(4, 4, 2, FW, 256)
    token = []

    def turn(kernel, *arguments, waited=()):
        *results, last = kernel([place, *token, *waited], *arguments)
        token[:] = [last]
        return results

    def along(axis, values, steps):
        return [lax.ppermute(value, "dp", axis[k]) for value, k in zip(values, steps)]

    def of_core(which):
        return lax.dynamic_index_in_dim(window, which, 2, keepdims=False)

    def z_start(n):
        to_1, kept = turn(z_sends, *common, arrived[n], got[n], last[n], n)
        return kept, lax.ppermute(to_1, "dp", Z[1])

    def z_end(kept, z_got):
        return [(kept, 0), (z_got, 0), (lax.ppermute(add(kept[1], z_got[1]).astype(bf16), "dp", Z[2]), None)]

    arrived, got, last = {}, {}, {}
    to_core = turn(core_rows, grads, (0, 2))
    arrived[0], arrived[2] = along({0: CORE}, to_core, (0, 0))
    theirs = lax.ppermute(of_core(1 - core), "dp", CORE)
    common = (grads, add(of_core(core), theirs).astype(bf16))
    arrived[1] = lax.ppermute(turn(core_rows, grads, (1,), waited=(theirs, arrived[2]))[0], "dp", CORE)
    got[0] = along(X, turn(first_sends, *common, arrived[0], 0), (1, 3))
    b_got = lax.ppermute(turn(z_first_sends, *common, arrived[2], 2)[0], "dp", Z[1])
    first = turn(first_sends, *common, arrived[1], 1)
    b_last = lax.ppermute(turn(z_second_sends, *common, arrived[2], b_got, 2)[0], "dp", Z[2])
    second = turn(second_sends, *common, arrived[0], got[0], 0)
    last[0] = along(X, second, (3, 1))
    got[1] = along(X, first, (1, 3))
    last[1] = along(X, turn(second_sends, *common, arrived[1], got[1], 1), (3, 1))
    pieces = [z_end(*z_start(0)), z_end(*z_start(1))]
    to_1, to_3, on_3, on_1, own = turn(x_later_sends, *common, arrived[2], (b_got, b_last), 2)
    got_1, got_3 = along(X, (to_1, to_3), (1, 3))
    on_3, on_1 = add(on_3, got_1[1]).astype(bf16), add(on_1, got_3[1]).astype(bf16)
    on_3, on_1 = along(X, (on_3, on_1), (3, 1))
    received = jnp.concatenate([got_1[0], got_3[0]], axis=0), jnp.concatenate([on_3, on_1], axis=0)
    pieces.append([(own, None), (received[0], None), (received[1], None)])
    nesterov, sums, mine, *others = turn(gram_packed, pieces)
    mine = add(mine, *(lax.ppermute(other, "shard", Y[k]) for k, other in zip((1, 2, 3), others))).astype(bf16)
    mine = add(mine, lax.ppermute(mine, "shard", Y[4])).astype(bf16)
    parts = [mine] + [lax.ppermute(mine, "shard", Y[k]) for k in (1, 2, 3)]
    update = turn(iterate, nesterov, parts)[0]
    momentum = (momentum_beta - JOIN) * scaled + exchange(sums.reshape(32, 22, 256)).astype(f32)
    return (exchange(update.reshape(32, 22, 256)), momentum)


def solution(mesh):
    in_specs = (P("dp", None, None, "shard"), P(None, "dp", "shard"), P(None, "dp", "shard"))
    out_specs = (P(None, "dp", "shard"), P(None, "dp", "shard"))
    return jax.shard_map(local, mesh=mesh, in_specs=in_specs, out_specs=out_specs, check_vma=False)
```

```python
import math

import jax
import jax.numpy as jnp
from jax import lax
from jax.experimental import pallas as pl
from jax.experimental.pallas import tpu as pltpu
from jax.sharding import PartitionSpec as P

D = 2048
FW = 704
BLK = 32
ITERS = 3

coef_a = 3.4445
coef_b = -4.775
coef_c = 2.0315
momentum_beta = 0.95
epsilon = 1e-07
bf16 = jnp.bfloat16
f32 = jnp.float32

CHUNKS = (144,112,96)
STARTS = [2 * sum(CHUNKS[:n]) for n in range(len(CHUNKS))]
PAD = 768
JOIN = momentum_beta * momentum_beta / (1 + momentum_beta)
WINDOW = 64


def dp_moves(move):
    pairs = []
    for x in range(4):
        for z in range(4):
            for core in range(2):
                nx, nz, nc = move(x, z, core)
                pairs.append((x * 8 + z * 2 + core, nx * 8 + nz * 2 + nc))
    return pairs


CORE = dp_moves(lambda x, z, core: (x, z, 1 - core))
X = {k: dp_moves(lambda x, z, core, k=k: (x ^ k, z, core)) for k in (1, 3)}
Z = {k: dp_moves(lambda x, z, core, k=k: (x, z ^ k, core)) for k in (1, 2)}
Y = {k: [(s, s ^ k) for s in range(8)] for k in (1, 2, 3, 4)}


def add(*terms):
    total = terms[0].astype(f32)
    for term in terms[1:]:
        total = total + term.astype(f32)
    return total


LARGE = 50 * 2**20
VMEM = 14 * 2**20


TOKEN = jax.ShapeDtypeStruct((16, 128), bf16)


def call(body, place, operands, outs, scratch, flops=0, vmem=VMEM, space=pltpu.VMEM):
    place, *waited = place
    first = 1 + len(operands)

    def with_token(*refs):
        rest = refs[first + len(waited) :]
        token = rest[len(outs)]
        token[...] = jnp.zeros_like(token)
        body(*refs[:first], *rest[: len(outs)], *rest[len(outs) + 1 :])

    return pl.pallas_call(
        with_token,
        out_shape=[jax.ShapeDtypeStruct(shape, bf16) for shape in outs] + [TOKEN],
        in_specs=[pl.BlockSpec(memory_space=pltpu.SMEM)] + [pl.BlockSpec(memory_space=pl.ANY)] * (first - 1 + len(waited)),
        out_specs=[pl.BlockSpec(memory_space=space)] * len(outs) + [pl.BlockSpec(memory_space=pltpu.VMEM)],
        scratch_shapes=scratch,
        compiler_params=pltpu.CompilerParams(vmem_limit_bytes=vmem),
        cost_estimate=pl.CostEstimate(flops=flops, bytes_accessed=6000000, transcendentals=0),
    )(place, *operands, *waited)


def begin(pairs, sems):
    copies = [pltpu.make_async_copy(source, target, sems.at[n]) for n, (source, target) in enumerate(pairs)]
    for copy in copies:
        copy.start()
    return copies


def finish(copies):
    for copy in copies:
        copy.wait()


def core_rows(place, grads, chunks):
    def body(place, grads, *refs):
        outs, buffers, (sems, out_sems) = refs[: len(chunks)], refs[len(chunks) : -2], refs[-2:]
        pairs, targets = [], []
        for n, out, buffer in zip(chunks, outs, buffers):
            rows = pl.ds(STARTS[n], 2 * CHUNKS[n])
            for x in range(4):
                pairs.append((grads.at[x, :, 1 - place[2], rows], buffer.at[x]))
                targets.append((buffer.at[x], out.at[x]))
        writes = []
        for n, read in enumerate(begin(pairs, sems)):
            read.wait()
            writes.append(pltpu.make_async_copy(*targets[n], out_sems.at[n]))
            writes[n].start()
        finish(writes)

    shapes = [(4, 4, 2 * CHUNKS[n], 256) for n in chunks]
    sems = [pltpu.SemaphoreType.DMA((4 * len(chunks),))] * 2
    return call(
        body, place, (grads,), shapes, [pltpu.VMEM(shape, bf16) for shape in shapes] + sems, vmem=LARGE, space=pl.ANY
    )


def tree_add(terms):
    while len(terms) > 1:
        terms = [sum(terms[n + 1 : n + 2], terms[n]) for n in range(0, len(terms), 2)]
    return terms[0]


def sums_kernel(place, grads, joined, arrived, others, outs, jobs, start, rows, along_x=False):
    count = len(jobs)
    terms = 2 + max(len(job[2]) for job in jobs)

    def body(place, grads, joined, arrived, *refs):
        others_in, refs = refs[: len(others)], refs[len(others) :]
        outs_ref, (buffers, window, sems) = refs[: len(outs)], refs[len(outs) :]
        x, z, core = place[0], place[1], place[2]
        reads = []
        for n, (k, first, extra, _) in enumerate(jobs):
            which = (slice(None), z ^ k) if along_x else (x ^ k, slice(None))
            pairs = [
                (grads.at[(*which, core, pl.ds(start + first, rows))], buffers.at[n, 0]),
                (joined.at[which], window.at[n]),
                (arrived.at[(*which, pl.ds(first, rows))], buffers.at[n, 1]),
            ]
            pairs += [(term(others_in), buffers.at[n, 2 + t]) for t, term in enumerate(extra)]
            reads.append(begin(pairs, sems.at[n]))
        for n, (k, first, extra, store) in enumerate(jobs):
            finish(reads[n])
            for i in range(WINDOW // 16):
                at = place[4] + 16 * i - start - first

                @pl.when((at >= 0) & (at < rows))
                def _(n=n, i=i, at=at):
                    there = pl.ds(pl.multiple_of(at, 16), 16)
                    buffers[n, 0, :, there] = add(buffers[n, 0, :, there], window[n, :, 16 * i : 16 * i + 16]).astype(bf16)

            store(outs_ref, lambda j: tree_add([buffers[n, t, j] for t in range(2 + len(extra))]), x, z)

    return call(
        body, place, (grads, joined, arrived, *others), outs,
        [
            pltpu.VMEM((count, terms, 4, rows, 256), bf16),
            pltpu.VMEM((count, 4, WINDOW, 256), bf16),
            pltpu.SemaphoreType.DMA((count, terms + 1)),
        ],
        vmem=LARGE,
    )


def first_sends(place, grads, joined, arrived, n):
    half = CHUNKS[n]

    def job(k, part, slot):
        def store(outs, value, x, z):
            for j in range(4):
                outs[part][slot, j] = value(j)

        return (k, part * half, [], store)

    jobs = [job(2, 0, 1), job(1, 0, 0), job(2, 1, 1), job(3, 1, 0)]
    return sums_kernel(place, grads, joined, arrived, (), [(2, 4, half, 256)] * 2, jobs, STARTS[n], half)


def second_sends(place, grads, joined, arrived, got, n):
    half = CHUNKS[n]

    def job(k, part):
        def store(outs, value, x, z):
            for j in range(4):
                outs[part][j] = value(j)

        return (k, part * half, [lambda refs: refs[part].at[1]], store)

    return sums_kernel(
        place, grads, joined, arrived, got, [(4, half, 256)] * 2, [job(3, 0), job(1, 1)], STARTS[n], half
    )


def z_sends(place, grads, joined, arrived, got, last, n):
    half = CHUNKS[n]

    def job(part):
        def store(outs, value, x, z):
            rows = slice(part * half, part * half + half)
            for out, slot, k in ((0, 0, 1), (0, 1, 3), (1, 0, 0), (1, 1, 2)):
                outs[out][slot, rows] = value(z ^ k)

        return (0, part * half, [lambda refs: refs[part].at[0], lambda refs: refs[2 + part]], store)

    return sums_kernel(
        place, grads, joined, arrived, (*got, *last), [(2, 2 * half, 256)] * 2, [job(0), job(1)], STARTS[n], half
    )


def z_first_sends(place, grads, joined, arrived, n):
    def job(k, slot):
        def store(outs, value, x, z):
            for j in range(4):
                outs[0][slot, j] = value(j)

        return (k, 0, [], store)

    rows = 2 * CHUNKS[n]
    return sums_kernel(
        place, grads, joined, arrived, (), [(2, 4, rows, 256)], [job(1, 0), job(3, 1)], STARTS[n], rows, along_x=True
    )


def z_second_sends(place, grads, joined, arrived, got, n):
    def store(outs, value, x, z):
        for j in range(4):
            outs[0][j] = value(j)

    rows = 2 * CHUNKS[n]
    job = (2, 0, [lambda refs: refs[0].at[1]], store)
    return sums_kernel(place, grads, joined, arrived, (got,), [(4, rows, 256)], [job], STARTS[n], rows, along_x=True)


def x_later_sends(place, grads, joined, arrived, got, n):
    half = CHUNKS[n]

    def store(outs, value, x, z):
        to_1, to_3, on_3, on_1, own = outs
        far = value(x ^ 2)
        to_1[1], to_3[1] = far[:half], far[half:]
        near = value(x ^ 1)
        to_1[0], on_1[...] = near[:half], near[half:]
        near = value(x ^ 3)
        on_3[...], to_3[0] = near[:half], near[half:]
        own[...] = value(x)

    extra = [lambda refs: refs[0].at[0], lambda refs: refs[1]]
    outs = [(2, half, 256)] * 2 + [(half, 256)] * 2 + [(2 * half, 256)]
    return sums_kernel(
        place, grads, joined, arrived, got, outs, [(0, 0, extra, store)], STARTS[n], 2 * half, along_x=True
    )


def dot_t(a, b):
    return lax.dot_general(a, b, (((1,), (1,)), ((), ())), preferred_element_type=f32)


def dot(a, b):
    return jnp.dot(a, b, preferred_element_type=f32)


PACKED = 7 * 128


def packed_blocks():
    for i in range(3):
        pieces = []
        for r in range(4):
            part, at = divmod(128 * i + 32 * r, 96)
            pieces.append((part, slice(at, at + 32), slice(32 * r, 32 * r + 32)))
        yield i, slice(0, 128 * (i + 1)), pieces
        yield 5 - i, slice(128 * (i + 1), PACKED), pieces


def gram_packed(place, pieces):
    count = len(CHUNKS)

    def body(place, *refs):
        total = sum(len(piece) for piece in pieces)
        parts, refs = refs[:total], refs[total:]
        nesterov, sums, outs, (padded, packed, held, sems) = refs[0], refs[1], refs[2:6], refs[6:]
        reads = []
        for n in range(count):
            rows = pl.ds(STARTS[n], 2 * CHUNKS[n])
            sources = [part if slot is None else part.at[slot] for part, (_, slot) in zip(parts[3 * n : 3 * n + 3], pieces[n])]
            reads.append(begin([(source, held.at[k, rows]) for k, source in enumerate(sources)], sems.at[n]))
        padded[FW:] = jnp.zeros((PAD - FW, 256), bf16)
        for n in range(count):
            finish(reads[n])
            rows = slice(STARTS[n], STARTS[n] + 2 * CHUNKS[n])
            mean = add(*(held[k, rows] for k in range(3))) * (1 / 32)
            value = ((1 + momentum_beta) * mean).astype(bf16)
            sums[rows] = mean.astype(bf16)
            nesterov[rows] = value
            padded[rows] = value
        for j, where, places in packed_blocks():
            block = dot_t(padded[128 * j : 128 * j + 128], padded[: 128 * (j + 1)]).astype(bf16)
            for part, rows, inside in places:
                packed[part, rows, where] = block[inside]
        for k in range(4):
            outs[k][...] = packed[place[3] ^ k]

    return call(
        body, place, [part for piece in pieces for part, _ in piece], [(FW, 256)] * 2 + [(96, PACKED)] * 4,
        [
            pltpu.VMEM((PAD, 256), bf16), pltpu.VMEM((4, 96, PACKED), bf16), pltpu.VMEM((3, FW, 256), bf16),
            pltpu.SemaphoreType.DMA((count, 3)),
        ],
    )


def iterate(place, nesterov, parts):
    scale_factor = 0.2 * math.sqrt(max(D, FW))

    def body(place, nesterov, part_0, part_1, part_2, part_3, result, packed, gram, other, mixing, current, applied, held, sems):
        parts = (part_0, part_1, part_2, part_3)
        reads = begin([(part, packed.at[place[3] ^ k]) for k, part in enumerate(parts)] + [(nesterov, held)], sems)
        current[FW:] = jnp.zeros((PAD - FW, 256), bf16)
        finish(reads)
        total = jnp.zeros((128, 128), f32)
        eye = lax.broadcasted_iota(jnp.int32, (128, 128), 0) == lax.broadcasted_iota(jnp.int32, (128, 128), 1)
        for j, where, places in packed_blocks():
            for part, rows, inside in places:
                gram[128 * j + inside.start : 128 * j + inside.stop, : 128 * (j + 1)] = packed[part, rows, where]
            total = total + jnp.where(eye, gram[128 * j : 128 * j + 128, 128 * j : 128 * j + 128].astype(f32), 0.0)
        inverse = 1.0 / (jnp.sqrt(jnp.sum(total)) + epsilon)
        squared = inverse * inverse
        for j in range(6):
            for l in range(j + 1):
                down, across = slice(128 * j, 128 * j + 128), slice(128 * l, 128 * l + 128)
                block = gram[down, across].astype(f32) * squared
                gram[down, across] = block.astype(bf16)
                if l < j:
                    gram[across, down] = block.T.astype(bf16)
        tiles = [slice(256 * n, 256 * n + 256) for n in range(3)]
        current[:FW] = (held[...].astype(f32) * inverse).astype(bf16)
        for iteration in range(ITERS):
            if iteration == ITERS - 1:
                for t in tiles:
                    applied[t] = dot(gram[t], current[...]).astype(bf16)
                for n, t in enumerate(tiles):
                    value = coef_a * current[t].astype(f32) + coef_b * applied[t].astype(f32)
                    value = scale_factor * (value + coef_c * dot(gram[t], applied[...]))
                    rows = slice(256 * n, min(256 * n + 256, FW))
                    result[rows] = value.astype(bf16)[: rows.stop - rows.start]
                break
            for t in tiles:
                mixing[t] = (coef_b * gram[t].astype(f32) + coef_c * dot(gram[t], gram[...])).astype(bf16)
            moved = [coef_a * current[t].astype(f32) + dot(mixing[t], current[...]) for t in tiles]
            for n, t in enumerate(tiles):
                current[t] = moved[n].astype(bf16)
            for t in tiles:
                other[t] = dot(mixing[t], gram[...]).astype(bf16)
            for t in tiles:
                gram[t] = (
                    coef_a * coef_a * gram[t].astype(f32) + 2 * coef_a * other[t].astype(f32) + dot(other[t], mixing[...])
                ).astype(bf16)

    square = pltpu.VMEM((PAD, PAD), bf16)
    return call(
        body, place, [nesterov, *parts], [(FW, 256)],
        [
            pltpu.VMEM((4, 96, PACKED), bf16), square, square, square,
            pltpu.VMEM((PAD, 256), bf16), pltpu.VMEM((PAD, 256), bf16), pltpu.VMEM((FW, 256), bf16),
            pltpu.SemaphoreType.DMA((5,)),
        ],
        flops=8 * 10**9,
    )


def exchange(values):
    return lax.all_to_all(values, "dp", split_axis=0, concat_axis=0, tiled=True)


def window_rows(scaled, core, chip, low):
    at = jnp.arange(WINDOW)[:, None] - (44 * chip + 22 * core - low)
    move = (at == jnp.arange(22)[None, :]).astype(bf16)
    weighted = (32 * JOIN * scaled).astype(bf16)
    moved = jnp.einsum("wr,mrc->mwc", move, weighted, preferred_element_type=f32).astype(bf16)
    return moved.reshape(4, 4, 2, WINDOW, 256)


def local(grads, mantissa, exponents):
    d = lax.axis_index("dp")
    shard = lax.axis_index("shard")
    chip, core = d // 2, d % 2
    low = jnp.minimum(44 * chip // 16 * 16, FW - WINDOW)
    place = jnp.stack([chip // 4, chip % 4, core, shard % 4, low]).astype(jnp.int32)
    spread = (jnp.arange(256)[None, :] // BLK == jnp.arange(256 // BLK)[:, None]).astype(bf16)
    scales = jnp.einsum("mrb,bc->mrc", jnp.exp2(exponents.astype(f32)).astype(bf16), spread, preferred_element_type=f32)
    scaled = mantissa.astype(f32) * scales
    window = window_rows(scaled, core, chip, low)
    grads = grads[0].reshape(4, 4, 2, FW, 256)
    token = []

    def turn(kernel, *arguments, waited=()):
        *results, last = kernel([place, *token, *waited], *arguments)
        token[:] = [last]
        return results

    def along(axis, values, steps):
        return [lax.ppermute(value, "dp", axis[k]) for value, k in zip(values, steps)]

    def of_core(which):
        return lax.dynamic_index_in_dim(window, which, 2, keepdims=False)

    def z_start(n):
        to_1, kept = turn(z_sends, *common, arrived[n], got[n], last[n], n)
        return kept, lax.ppermute(to_1, "dp", Z[1])

    def z_end(kept, z_got):
        return [(kept, 0), (z_got, 0), (lax.ppermute(add(kept[1], z_got[1]).astype(bf16), "dp", Z[2]), None)]

    arrived, got, last = {}, {}, {}
    to_core = turn(core_rows, grads, (0, 2))
    arrived[0], arrived[2] = along({0: CORE}, to_core, (0, 0))
    theirs = lax.ppermute(of_core(1 - core), "dp", CORE)
    common = (grads, add(of_core(core), theirs).astype(bf16))
    arrived[1] = lax.ppermute(turn(core_rows, grads, (1,), waited=(theirs, arrived[2]))[0], "dp", CORE)
    got[0] = along(X, turn(first_sends, *common, arrived[0], 0), (1, 3))
    b_got = lax.ppermute(turn(z_first_sends, *common, arrived[2], 2)[0], "dp", Z[1])
    first = turn(first_sends, *common, arrived[1], 1)
    second = turn(second_sends, *common, arrived[0], got[0], 0)
    last[0] = along(X, second, (3, 1))
    b_last = lax.ppermute(turn(z_second_sends, *common, arrived[2], b_got, 2)[0], "dp", Z[2])
    got[1] = along(X, first, (1, 3))
    last[1] = along(X, turn(second_sends, *common, arrived[1], got[1], 1), (3, 1))
    pieces = [z_end(*z_start(0)), z_end(*z_start(1))]
    to_1, to_3, on_3, on_1, own = turn(x_later_sends, *common, arrived[2], (b_got, b_last), 2)
    got_1, got_3 = along(X, (to_1, to_3), (1, 3))
    on_3, on_1 = add(on_3, got_1[1]).astype(bf16), add(on_1, got_3[1]).astype(bf16)
    on_3, on_1 = along(X, (on_3, on_1), (3, 1))
    received = jnp.concatenate([got_1[0], got_3[0]], axis=0), jnp.concatenate([on_3, on_1], axis=0)
    pieces.append([(own, None), (received[0], None), (received[1], None)])
    nesterov, sums, mine, *others = turn(gram_packed, pieces)
    mine = add(mine, *(lax.ppermute(other, "shard", Y[k]) for k, other in zip((1, 2, 3), others))).astype(bf16)
    mine = add(mine, lax.ppermute(mine, "shard", Y[4])).astype(bf16)
    parts = [mine] + [lax.ppermute(mine, "shard", Y[k]) for k in (1, 2, 3)]
    update = turn(iterate, nesterov, parts)[0]
    momentum = (momentum_beta - JOIN) * scaled + exchange(sums.reshape(32, 22, 256)).astype(f32)
    return (exchange(update.reshape(32, 22, 256)), momentum)


def solution(mesh):
    in_specs = (P("dp", None, None, "shard"), P(None, "dp", "shard"), P(None, "dp", "shard"))
    out_specs = (P(None, "dp", "shard"), P(None, "dp", "shard"))
    return jax.shard_map(local, mesh=mesh, in_specs=in_specs, out_specs=out_specs, check_vma=False)
```
